32 devices in a mesh: row: 4 (over y, x), col: 4 (over z), depth: 2 (over core).
Axes of the slice: x: 2, y: 2, z: 4, core: 2. Of those that a mesh axis runs over, the one named last changes fastest.
Arguments:
- left_block_slots: bfloat16 [4, 4, 2, 1, 16, 128, 128], P('row', 'col', 'depth'), may hold values from -6 to 6
- a_index: int32 [4, 4, 2, 1, 16], P('row', 'col', 'depth'), may hold values from 0 to 31, as said below
- a_count: int32 [4, 4, 2, 1], P('row', 'col', 'depth'), may hold values from 4 to 16, as said below
- b_blocks: bfloat16 [4, 4, 2, 1, 8, 128, 128], P('row', 'col', 'depth'), may hold values from -0.1875 to 0.1875
- b_index: int32 [4, 4, 2, 1, 8], P('row', 'col', 'depth'), may hold values from 0 to 63, as said below
- b_count: int32 [4, 4, 2, 1], P('row', 'col', 'depth'), may hold values from 2 to 8, as said below
- c_index: int32 [4, 4, 24], P('row', 'col'), may hold values from 0 to 31, as said below
Outputs:
- c_blocks: bfloat16 [4, 4, 24, 128, 128], P('row', 'col', 'depth')
The draws below stay inside these ranges and needn't reach their ends.
Inputs may be any that keep to these rules, and one draw needn't show every extreme that they name: `a_index`: within one panel the live positions are distinct. `a_count`: some panel has all 16 slots live. `b_index`: within one panel the live positions are distinct. `b_count`: some panel has all 8 slots live. `c_index`: within one panel the positions are distinct.
All inputs are finite; a program needn't handle non-finite values.
Results may differ from the reference program's by a relative error of at most 0.001.
Values may be sent and summed in bfloat16 or wider, within the bound.
A program may use at most 128 MiB of HBM per device.

```python
import jax
import jax.numpy as jnp
from jax import lax

BS = 128
RB = 4
KB = 8
CB = 8
NNZ_A = 16
NNZ_B = 8
NNZ_C = 24
SPAN = 4
MA = 1
MB = 1
N_ROW = 4
N_COL = 4
N_DEPTH = 2


def distinct_positions(key, lead, product_total, keep):
    scores = jax.random.randint(key, lead + (product_total,), 0, 65536) * product_total + jnp.arange(product_total, dtype=jnp.int32)
    order = jnp.argsort(scores, axis=-1, stable=True)
    return order[..., :keep].astype(jnp.int32)


def live_counts(key, lead, most):
    counts = jax.random.randint(key, lead, most // 4, most + 1).reshape(-1)
    counts = counts.at[0].set(most)
    return counts.reshape(lead).astype(jnp.int32)


def draw_a_index(key, part):
    key = jax.random.fold_in(key, 11)
    return distinct_positions(key, (N_ROW, N_COL, N_DEPTH, MA), RB * KB, NNZ_A)


def draw_a_count(key, part):
    key = jax.random.fold_in(key, 12)
    return live_counts(key, (N_ROW, N_COL, N_DEPTH, MA), NNZ_A)


def draw_b_index(key, part):
    key = jax.random.fold_in(key, 13)
    return distinct_positions(key, (N_ROW, N_COL, N_DEPTH, MB), KB * CB, NNZ_B)


def draw_b_count(key, part):
    key = jax.random.fold_in(key, 14)
    return live_counts(key, (N_ROW, N_COL, N_DEPTH, MB), NNZ_B)


def draw_c_index(key, part):
    key = jax.random.fold_in(key, 15)
    return distinct_positions(key, (N_ROW, N_COL), RB * CB, NNZ_C)


def level_of(rng, extent, shards, smallest, high):
    loudness, own = 1.0, jax.random.fold_in(rng, 6)
    for axis_at, shards_of in shards:
        draws = jnp.exp(jax.random.uniform(jax.random.fold_in(own, axis_at), (shards_of,), jnp.float32, smallest / len(shards), high / len(shards)))
        loudness = loudness * jnp.repeat(draws, extent[axis_at] // shards_of).reshape([-1 if axis == axis_at else 1 for axis in range(len(extent))])
    return loudness


def normal_values(key, extent, deviation, reach, cuts=(), kind=jnp.bfloat16):
    factor_of = level_of(key, extent, cuts, -0.22, 0.18) if cuts else 1.0
    values = jax.random.normal(key, extent, jnp.float32) * deviation * factor_of
    return jnp.minimum(jnp.maximum(values, -reach), reach).astype(kind)


def setup_inputs(seed: int = 0) -> dict:
    key_list = jax.random.split(jax.random.key(seed), 8)
    left_block_slots = normal_values(key_list[0], (N_ROW, N_COL, N_DEPTH, MA, NNZ_A, BS, BS), 1.0, 6.0, ((0, 4), (1, 4), (2, 2)))
    a_index = draw_a_index(jax.random.fold_in(key_list[7], 71), 0)
    a_count = draw_a_count(jax.random.fold_in(key_list[7], 71), 0)
    b_blocks = normal_values(key_list[3], (N_ROW, N_COL, N_DEPTH, MB, NNZ_B, BS, BS), (SPAN * N_DEPTH * BS) ** -0.5, 0.1875, ((0, 4), (1, 4), (2, 2)))
    b_index = draw_b_index(jax.random.fold_in(key_list[7], 71), 0)
    b_count = draw_b_count(jax.random.fold_in(key_list[7], 71), 0)
    c_index = draw_c_index(jax.random.fold_in(key_list[7], 71), 0)
    return dict(left_block_slots=left_block_slots, a_index=a_index, a_count=a_count, b_blocks=b_blocks, b_index=b_index, b_count=b_count, c_index=c_index)


def expand_to_full(blocks, positions, count, grid):
    slots = blocks.shape[0]
    live = jnp.arange(slots, dtype=jnp.int32) < count
    picker = ((positions[None, :] == jnp.arange(grid, dtype=jnp.int32)[:, None]) & live[None, :]).astype(jnp.bfloat16)
    flat = blocks.reshape(slots, -1)
    return jnp.dot(picker, flat, preferred_element_type=jnp.float32).astype(jnp.bfloat16)


def contribute(product_total, a_blk, a_pos, a_cnt, b_blk, b_pos, b_cnt, rows_t, cols_t):
    side = a_blk.shape[-1]
    dense_a = expand_to_full(a_blk, a_pos, a_cnt, RB * KB).reshape(RB, KB, side, side)
    right_full_matrix = expand_to_full(b_blk, b_pos, b_cnt, KB * CB).reshape(KB, CB, side, side)
    left_strip_panel = jnp.take(dense_a, rows_t, axis=0).astype(jnp.float32)
    right_strip_panel = jnp.take(right_full_matrix, cols_t, axis=1).astype(jnp.float32)
    return product_total + jnp.einsum("oxmn,xonw->omw", left_strip_panel, right_strip_panel)


def reference(left_block_slots, a_index, a_count, b_blocks, b_index, b_count, c_index):
    def panel(pair):
        rowp = pair // N_COL
        colp = pair % N_COL
        targets = c_index[rowp, colp]
        rows_t = targets // CB
        cols_t = targets % CB

        def one(product_total, inner):
            local = inner % SPAN
            layer = inner // SPAN
            col_a = (local - rowp) % N_COL
            slot_a = ((local - rowp - col_a) % SPAN) // N_COL
            row_b = (local - colp) % N_ROW
            slot_b = ((local - colp - row_b) % SPAN) // N_ROW
            product_total = contribute(product_total, left_block_slots[rowp, col_a, layer, slot_a], a_index[rowp, col_a, layer, slot_a],
                               a_count[rowp, col_a, layer, slot_a], b_blocks[row_b, colp, layer, slot_b],
                               b_index[row_b, colp, layer, slot_b], b_count[row_b, colp, layer, slot_b],
                               rows_t, cols_t)
            return product_total, None

        start = jnp.zeros((NNZ_C, BS, BS), jnp.float32)
        product_total, unused = lax.scan(one, start, jnp.arange(SPAN * N_DEPTH, dtype=jnp.int32))
        return product_total.astype(jnp.bfloat16)

    result = lax.map(panel, jnp.arange(N_ROW * N_COL, dtype=jnp.int32))
    return result.reshape(N_ROW, N_COL, NNZ_C, BS, BS)
```

```python
import jax
import jax.numpy as jnp
from jax import lax
from jax.experimental import pallas as pl
from jax.experimental.pallas import tpu as pltpu
from jax.sharding import PartitionSpec as P

RB = 4
KB = 8
CB = 8
NCH = 4
MESH = pl.DeviceIdType.MESH


def from_behind(value, axis, steps):
    count = lax.axis_size(axis)
    pairs = [(source, (source + steps) % count) for source in range(count)]
    return lax.ppermute(value, axis, pairs)


def select_blocks(blocks, positions, count, wanted):
    slots = blocks.shape[0]
    side = blocks.shape[-1]
    live = jnp.arange(slots, dtype=jnp.int32) < count
    picker = ((wanted.reshape(-1)[:, None] == positions[None, :]) & live[None, :]).astype(
        jnp.bfloat16
    )
    flat = blocks.reshape(slots, side * side)
    chosen = jnp.dot(picker, flat, preferred_element_type=jnp.float32).astype(jnp.bfloat16)
    return chosen.reshape(wanted.shape + (side, side))


def contribute(product_total, left_portion, b_part, left_pick, right_pick):
    left_strip = select_blocks(left_portion[0], left_portion[1], left_portion[2], left_pick)
    right_strip = select_blocks(b_part[0], b_part[1], b_part[2], right_pick)
    return product_total + jnp.einsum(
        "oxmn,oxnw->omw", left_strip, right_strip, preferred_element_type=jnp.float32
    )


def pick(held, index):
    return tuple((lax.dynamic_index_in_dim(member, index, 0, keepdims=False) for member in held))


def window(held, leading, slot_count):
    chosen = jnp.stack(
        [
            jnp.asarray(leading, jnp.int32) % slot_count,
            (jnp.asarray(leading, jnp.int32) + 1) % slot_count,
        ]
    )
    return tuple((jnp.take(member, chosen, axis=0) for member in held))


def body(left_block_slots, a_index, a_count, b_blocks, b_index, b_count, c_index):
    row_pos = lax.axis_index("row")
    n_row = lax.axis_size("row")
    n_col = lax.axis_size("col")
    span = max(n_row, n_col)
    a_slots = left_block_slots.shape[3]
    b_slots = b_blocks.shape[3]
    rounds = max(a_slots, b_slots)
    length = span // rounds
    targets = c_index[0, 0]
    rows_t = targets // CB
    cols_t = targets % CB
    inner_cols = jnp.arange(KB, dtype=jnp.int32)
    left_pick = rows_t[:, None] * KB + inner_cols[None, :]
    right_pick = inner_cols[None, :] * CB + cols_t[:, None]
    a_held = (left_block_slots[0, 0, 0], a_index[0, 0, 0], a_count[0, 0, 0])
    b_held = (b_blocks[0, 0, 0], b_index[0, 0, 0], b_count[0, 0, 0])

    def a_use(held):
        return pick(held, 0)

    def a_move(held):
        return tuple(from_behind((held[0], held[1], held[2]), "col", -1))

    def a_end(held):
        return a_move(held)

    def b_begin(held, rnd):
        if b_slots > 1:
            return window(b_held, rnd, b_slots)
        return held

    def b_use(held, step):
        if b_slots > 1:
            return pick(held, (row_pos + step) // n_row)
        return pick(held, 0)

    def right_shifted(held):
        return tuple(from_behind((held[0], held[1], held[2]), "row", -1))

    def b_end(held):
        if b_slots == 1:
            return right_shifted(held)
        return held

    b_start = b_begin(b_held, 0)

    def run_round(rnd, a_now, b_now, product_total):
        a_now = tuple(a_now)
        b_now = tuple(b_begin(b_now, rnd))

        def inner(step, carry):
            a_cur, b_cur, acc = carry
            acc = contribute(acc, a_use(a_cur), b_use(b_cur, step), left_pick, right_pick)
            return (tuple(a_move(a_cur)), tuple(right_shifted(b_cur)), acc)

        a_now, b_now, product_total = lax.fori_loop(
            0, length - 1, inner, (a_now, b_now, product_total)
        )
        product_total = contribute(
            product_total, a_use(a_now), b_use(b_now, length - 1), left_pick, right_pick
        )
        return (a_now, b_now, product_total)

    def full_round(rnd, carry):
        a_now, b_now, product_total = run_round(rnd, carry[0], carry[1], carry[2])
        return (tuple(a_end(a_now)), tuple(b_end(b_now)), product_total)

    side = left_block_slots.shape[-1]
    start = jnp.zeros((targets.shape[0], side, side), jnp.float32)
    a_last, b_last, product_total = lax.fori_loop(
        0, rounds - 1, full_round, (tuple(a_held), tuple(b_start), start)
    )
    a_last, b_last, product_total = run_round(rounds - 1, a_last, b_last, product_total)
    shares = lax.psum_scatter(product_total, "depth", scatter_dimension=0, tiled=True)
    return shares.astype(jnp.bfloat16)[None, None]


def fast_kernel(
    a_hbm, b_hbm, a_idx, a_cnt, b_idx, b_cnt, c_idx, out,
    own, low_one, high_one, two, far_parts, b_all, tab_a, tab_b, ind_a, ind_b, b_dense, a_dense, total, give, take,
    local_sem, ind_sem, a_send, a_recv, b_send, b_recv,
    ta_send, ta_recv, tb_send, tb_recv, x_send, x_recv,
):
    r = lax.axis_index("row")
    c = lax.axis_index("col")
    d = lax.axis_index("depth")
    n = 4
    slots_a, side = a_hbm.shape[0], a_hbm.shape[1]
    slots_b = b_hbm.shape[0]
    half_b = slots_b // 2
    rows = side // NCH
    mine = out.shape[0]
    x, y = r % 2, r // 2
    across = (y * 2 + (1 - x), (1 - y) * 2 + x)
    corner = (1 - y) * 2 + (1 - x)

    barrier = pltpu.get_barrier_semaphore()
    z_peers = [(c + s) % n for s in range(1, n)]
    r_peers = [(r + s) % n for s in range(1, n)]
    for z in z_peers:
        pl.semaphore_signal(barrier, inc=1, device_id=(r, z, d), device_id_type=MESH)
    for q in r_peers:
        pl.semaphore_signal(barrier, inc=1, device_id=(q, c, d), device_id_type=MESH)
    pl.semaphore_signal(barrier, inc=1, device_id=(r, c, 1 - d), device_id_type=MESH)

    load_a = pltpu.make_async_copy(a_hbm, own.at[pl.ds(0, slots_a)], local_sem.at[0])
    load_b = pltpu.make_async_copy(b_hbm, b_all.at[r, pl.ds(0, slots_b)], local_sem.at[1])
    load_a.start()
    load_b.start()

    lane = lax.broadcasted_iota(jnp.int32, (8, 128), 1)
    inv_a = jnp.full((8, 128), slots_a, jnp.int32)
    for s in range(slots_a):
        inv_a = jnp.where((lane == a_idx[s]) & (s < a_cnt[0]), s, inv_a)
    inv_b = jnp.full((8, 128), slots_b, jnp.int32)
    for s in range(slots_b):
        inv_b = jnp.where((lane == b_idx[s]) & (s < b_cnt[0]), s, inv_b)
    tab_a[c] = inv_a
    tab_b[r] = inv_b
    for p in range(n):
        b_all[p, slots_b] = jnp.zeros((side, side), b_all.dtype)
    for panel_ref in (own, low_one, high_one, two):
        panel_ref[slots_a] = jnp.zeros((side, side), panel_ref.dtype)
    for part_ref in far_parts:
        part_ref[slots_a] = jnp.zeros((rows, side), part_ref.dtype)

    def zero(t, carry):
        total[t] = jnp.zeros((side, side), jnp.float32)
        return carry

    lax.fori_loop(0, RB * CB, zero, 0)

    held = ((own, low_one, two), (own, high_one, two))

    def piece(way, delta, h):
        if delta == n - 1:
            return far_parts[h].at[pl.ds(0, slots_a)]
        return held[way][delta].at[pl.ds(0, slots_a), pl.ds(h * rows, rows)]

    def a_copy(way, delta, h):
        return pltpu.make_async_remote_copy(
            src_ref=piece(way, delta, h), dst_ref=piece(way, delta + 1, h),
            send_sem=a_send.at[way, delta, h], recv_sem=a_recv.at[way, delta, h],
            device_id=(r, (c + 1 - 2 * way + n) % n, d), device_id_type=MESH,
        )

    def b_copy(source, half, way, k):
        part = b_all.at[source, pl.ds(half * half_b, half_b)]
        return pltpu.make_async_remote_copy(
            src_ref=part, dst_ref=part,
            send_sem=b_send.at[way, k], recv_sem=b_recv.at[source, half],
            device_id=(across[way], c, d), device_id_type=MESH,
        )

    def ta_copy(s):
        return pltpu.make_async_remote_copy(
            src_ref=tab_a.at[c], dst_ref=tab_a.at[c],
            send_sem=ta_send.at[s], recv_sem=ta_recv.at[c],
            device_id=(r, z_peers[s], d), device_id_type=MESH,
        )

    def tb_copy(s):
        return pltpu.make_async_remote_copy(
            src_ref=tab_b.at[r], dst_ref=tab_b.at[r],
            send_sem=tb_send.at[s], recv_sem=tb_recv.at[r],
            device_id=(r_peers[s], c, d), device_id_type=MESH,
        )

    def wait_ta(source):
        pltpu.make_async_remote_copy(
            src_ref=tab_a.at[source], dst_ref=tab_a.at[source],
            send_sem=ta_send.at[0], recv_sem=ta_recv.at[source],
            device_id=(r, z_peers[0], d), device_id_type=MESH,
        ).wait_recv()

    def wait_tb(source):
        pltpu.make_async_remote_copy(
            src_ref=tab_b.at[source], dst_ref=tab_b.at[source],
            send_sem=tb_send.at[0], recv_sem=tb_recv.at[source],
            device_id=(r_peers[0], c, d), device_id_type=MESH,
        ).wait_recv()

    load_a.wait()
    load_b.wait()
    pl.semaphore_wait(barrier, 7)

    for s in range(n - 1):
        tb_copy(s).start()
        ta_copy(s).start()
    for h in range(NCH):
        if h == 0:
            b_copy(r, 0, 0, 0).start()
            b_copy(r, 1, 1, 0).start()
        if h == 1:
            b_copy(r, 1, 0, 1).start()
            b_copy(r, 0, 1, 1).start()

        @pl.when(c < n - 1)
        def _():
            a_copy(0, 0, h).start()

        @pl.when(c > 0)
        def _():
            a_copy(1, 0, h).start()

    b_copy(across[0], 0, 1, 2).wait_recv()
    b_copy(across[0], 0, 1, 2).start()
    b_copy(across[1], 1, 0, 2).wait_recv()
    b_copy(across[1], 1, 0, 2).start()

    for s in range(n - 1):
        wait_ta(z_peers[s])
        wait_tb(r_peers[s])
    fetch_a = pltpu.make_async_copy(tab_a, ind_a, ind_sem.at[0])
    fetch_b = pltpu.make_async_copy(tab_b, ind_b, ind_sem.at[1])
    fetch_a.start()
    fetch_b.start()
    fetch_a.wait()
    fetch_b.wait()

    def expand_b(source):
        partner = (r + source - c + n) % n

        def one(q, carry):
            for j in range(CB):
                block = b_all[partner, ind_b[partner, 0, q * CB + j]]
                b_dense[j // 2, pl.ds(pl.multiple_of(q * side, side), side), pl.ds(j % 2 * side, side)] = block
            return carry

        lax.fori_loop(0, KB, one, 0)

    def multiply(ref, source, h):
        height = ref.shape[1]
        at = pl.ds(h * height, height)
        for i in range(RB):
            for q in range(KB):
                a_dense[pl.ds(i * height, height), pl.ds(q * side, side)] = ref[
                    ind_a[source, 0, i * KB + q]
                ]

        def one(t, carry):
            got = jnp.dot(
                a_dense[pl.ds(0, RB * height)], b_dense[t], preferred_element_type=jnp.float32
            )
            for i in range(RB):
                for j in range(2):
                    total[i * CB + t * 2 + j, at] += got[
                        i * height : (i + 1) * height, j * side : (j + 1) * side
                    ]
            return carry

        lax.fori_loop(0, CB // 2, one, 0)

    b_copy(across[0], 1, 0, 0).wait_recv()
    b_copy(across[1], 0, 0, 0).wait_recv()
    b_copy(corner, 0, 0, 0).wait_recv()
    b_copy(corner, 1, 0, 0).wait_recv()

    expand_b(c)
    multiply(own, c, 0)

    for delta in (1, 2):
        behind = (c - delta, c + delta)
        there = (behind[0] >= 0, behind[1] < n)
        onward = (c < n - 1, c > 0)
        for h in range(NCH):
            for way in range(2):

                @pl.when(there[way])
                def _():
                    a_copy(way, delta - 1, h).wait_recv()

                    @pl.when(onward[way])
                    def _():
                        a_copy(way, delta, h).start()

        if delta == 1:
            for way in range(2):

                @pl.when(there[way])
                def _():
                    expand_b(behind[way])
                    multiply(held[way][1], behind[way], 0)

        else:
            source = jnp.where(there[0], behind[0], behind[1])
            expand_b(source)
            multiply(two, source, 0)

    far = n - 1 - c
    is_end = (c == 0) | (c == n - 1)

    @pl.when(is_end)
    def _():
        expand_b(far)

    def x_copy(h):
        return pltpu.make_async_remote_copy(
            src_ref=give.at[h], dst_ref=take.at[h],
            send_sem=x_send.at[h], recv_sem=x_recv.at[h],
            device_id=(r, c, 1 - d), device_id_type=MESH,
        )

    def finish(h):
        at = pl.ds(h * rows, rows)
        x_copy(h).wait_recv()
        for t in range(mine):
            out[t, at] = (total[c_idx[d * mine + t], at] + take[h, t]).astype(out.dtype)

    for h in range(NCH):
        at = pl.ds(h * rows, rows)
        for way in range(2):

            @pl.when(c == (n - 1) * (1 - way))
            def _():
                a_copy(way, n - 2, h).wait_recv()

        @pl.when(is_end)
        def _():
            multiply(far_parts[h], far, h)

        for t in range(mine):
            give[h, t] = total[c_idx[(1 - d) * mine + t], at]
        x_copy(h).start()
        if h > 0:
            finish(h - 1)
    finish(NCH - 1)

    for h in range(NCH):
        x_copy(h).wait_send()
        for way in range(2):
            for delta in range(n - 1):
                has = (c >= delta) & (c < n - 1) if way == 0 else (c + delta < n) & (c > 0)

                @pl.when(has)
                def _():
                    a_copy(way, delta, h).wait_send()

    for way in range(2):
        for k in range(3):
            b_copy(r, 0, way, k).wait_send()
    for s in range(n - 1):
        ta_copy(s).wait_send()
        tb_copy(s).wait_send()


def fast_body(left_block_slots, a_index, a_count, b_blocks, b_index, b_count, c_index):
    slots_a, side = left_block_slots.shape[4], left_block_slots.shape[5]
    slots_b = b_blocks.shape[4]
    targets = c_index.shape[2]
    mine = targets // 2
    n = 4
    bf, f32, i32 = jnp.bfloat16, jnp.float32, jnp.int32
    rows = side // NCH
    dma = pltpu.SemaphoreType.DMA
    smem = pl.BlockSpec(memory_space=pltpu.SMEM)
    hbm = pl.BlockSpec(memory_space=pl.ANY)
    flops = 2 * RB * KB * CB * side**3 * n
    out = pl.pallas_call(
        fast_kernel,
        out_shape=jax.ShapeDtypeStruct((mine, side, side), bf),
        in_specs=[hbm, hbm, smem, smem, smem, smem, smem],
        out_specs=pl.BlockSpec(memory_space=pltpu.VMEM),
        scratch_shapes=[
            pltpu.VMEM((slots_a + 1, side, side), bf),
            pltpu.VMEM((slots_a + 1, side, side), bf),
            pltpu.VMEM((slots_a + 1, side, side), bf),
            pltpu.VMEM((slots_a + 1, side, side), bf),
            tuple(pltpu.VMEM((slots_a + 1, rows, side), bf) for h in range(NCH)),
            pltpu.VMEM((n, slots_b + 1, side, side), bf),
            pltpu.VMEM((n, 8, 128), i32),
            pltpu.VMEM((n, 8, 128), i32),
            pltpu.SMEM((n, 8, 128), i32),
            pltpu.SMEM((n, 8, 128), i32),
            pltpu.VMEM((CB // 2, KB * side, 2 * side), bf),
            pltpu.VMEM((RB * side, KB * side), bf),
            pltpu.VMEM((RB * CB, side, side), f32),
            pltpu.VMEM((NCH, mine, rows, side), f32),
            pltpu.VMEM((NCH, mine, rows, side), f32),
            dma((2,)),
            dma((2,)),
            dma((2, n - 1, NCH)),
            dma((2, n - 1, NCH)),
            dma((2, 3)),
            dma((n, 2)),
            dma((n - 1,)),
            dma((n,)),
            dma((n - 1,)),
            dma((n,)),
            dma((NCH,)),
            dma((NCH,)),
        ],
        compiler_params=pltpu.CompilerParams(
            collective_id=0, has_side_effects=True, vmem_limit_bytes=32 * 1024 * 1024
        ),
        cost_estimate=pl.CostEstimate(flops=flops, bytes_accessed=4 << 20, transcendentals=0),
    )(
        left_block_slots[0, 0, 0, 0],
        b_blocks[0, 0, 0, 0],
        a_index[0, 0, 0, 0],
        a_count[0, 0, 0],
        b_index[0, 0, 0, 0],
        b_count[0, 0, 0],
        c_index[0, 0],
    )
    return out[None, None]


def solution(mesh):
    placed = (
        P("row", "col", "depth", None, None, None, None),
        P("row", "col", "depth", None, None),
        P("row", "col", "depth", None),
        P("row", "col", "depth", None, None, None, None),
        P("row", "col", "depth", None, None),
        P("row", "col", "depth", None),
        P("row", "col", None),
    )
    square = (mesh.shape["row"], mesh.shape["col"], mesh.shape["depth"]) == (4, 4, 2)
    return jax.shard_map(
        fast_body if square else body,
        mesh=mesh,
        in_specs=placed,
        out_specs=P("row", "col", "depth", None, None),
        check_vma=False,
    )
```

```python
import jax
import jax.numpy as jnp
from jax import lax
from jax.experimental import pallas as pl
from jax.experimental.pallas import tpu as pltpu
from jax.sharding import PartitionSpec as P

RB = 4
KB = 8
CB = 8
NCH = 4
MESH = pl.DeviceIdType.MESH


def from_behind(value, axis, steps):
    count = lax.axis_size(axis)
    pairs = [(source, (source + steps) % count) for source in range(count)]
    return lax.ppermute(value, axis, pairs)


def select_blocks(blocks, positions, count, wanted):
    slots = blocks.shape[0]
    side = blocks.shape[-1]
    live = jnp.arange(slots, dtype=jnp.int32) < count
    picker = ((wanted.reshape(-1)[:, None] == positions[None, :]) & live[None, :]).astype(
        jnp.bfloat16
    )
    flat = blocks.reshape(slots, side * side)
    chosen = jnp.dot(picker, flat, preferred_element_type=jnp.float32).astype(jnp.bfloat16)
    return chosen.reshape(wanted.shape + (side, side))


def contribute(product_total, left_portion, b_part, left_pick, right_pick):
    left_strip = select_blocks(left_portion[0], left_portion[1], left_portion[2], left_pick)
    right_strip = select_blocks(b_part[0], b_part[1], b_part[2], right_pick)
    return product_total + jnp.einsum(
        "oxmn,oxnw->omw", left_strip, right_strip, preferred_element_type=jnp.float32
    )


def pick(held, index):
    return tuple((lax.dynamic_index_in_dim(member, index, 0, keepdims=False) for member in held))


def window(held, leading, slot_count):
    chosen = jnp.stack(
        [
            jnp.asarray(leading, jnp.int32) % slot_count,
            (jnp.asarray(leading, jnp.int32) + 1) % slot_count,
        ]
    )
    return tuple((jnp.take(member, chosen, axis=0) for member in held))


def body(left_block_slots, a_index, a_count, b_blocks, b_index, b_count, c_index):
    row_pos = lax.axis_index("row")
    n_row = lax.axis_size("row")
    n_col = lax.axis_size("col")
    span = max(n_row, n_col)
    a_slots = left_block_slots.shape[3]
    b_slots = b_blocks.shape[3]
    rounds = max(a_slots, b_slots)
    length = span // rounds
    targets = c_index[0, 0]
    rows_t = targets // CB
    cols_t = targets % CB
    inner_cols = jnp.arange(KB, dtype=jnp.int32)
    left_pick = rows_t[:, None] * KB + inner_cols[None, :]
    right_pick = inner_cols[None, :] * CB + cols_t[:, None]
    a_held = (left_block_slots[0, 0, 0], a_index[0, 0, 0], a_count[0, 0, 0])
    b_held = (b_blocks[0, 0, 0], b_index[0, 0, 0], b_count[0, 0, 0])

    def a_use(held):
        return pick(held, 0)

    def a_move(held):
        return tuple(from_behind((held[0], held[1], held[2]), "col", -1))

    def a_end(held):
        return a_move(held)

    def b_begin(held, rnd):
        if b_slots > 1:
            return window(b_held, rnd, b_slots)
        return held

    def b_use(held, step):
        if b_slots > 1:
            return pick(held, (row_pos + step) // n_row)
        return pick(held, 0)

    def right_shifted(held):
        return tuple(from_behind((held[0], held[1], held[2]), "row", -1))

    def b_end(held):
        if b_slots == 1:
            return right_shifted(held)
        return held

    b_start = b_begin(b_held, 0)

    def run_round(rnd, a_now, b_now, product_total):
        a_now = tuple(a_now)
        b_now = tuple(b_begin(b_now, rnd))

        def inner(step, carry):
            a_cur, b_cur, acc = carry
            acc = contribute(acc, a_use(a_cur), b_use(b_cur, step), left_pick, right_pick)
            return (tuple(a_move(a_cur)), tuple(right_shifted(b_cur)), acc)

        a_now, b_now, product_total = lax.fori_loop(
            0, length - 1, inner, (a_now, b_now, product_total)
        )
        product_total = contribute(
            product_total, a_use(a_now), b_use(b_now, length - 1), left_pick, right_pick
        )
        return (a_now, b_now, product_total)

    def full_round(rnd, carry):
        a_now, b_now, product_total = run_round(rnd, carry[0], carry[1], carry[2])
        return (tuple(a_end(a_now)), tuple(b_end(b_now)), product_total)

    side = left_block_slots.shape[-1]
    start = jnp.zeros((targets.shape[0], side, side), jnp.float32)
    a_last, b_last, product_total = lax.fori_loop(
        0, rounds - 1, full_round, (tuple(a_held), tuple(b_start), start)
    )
    a_last, b_last, product_total = run_round(rounds - 1, a_last, b_last, product_total)
    shares = lax.psum_scatter(product_total, "depth", scatter_dimension=0, tiled=True)
    return shares.astype(jnp.bfloat16)[None, None]


def fast_kernel(
    a_hbm, b_hbm, a_idx, a_cnt, b_idx, b_cnt, c_idx, out,
    own, near, other, far, b_mine, b_mate, tab_a, tab_b, tab_e, ind_a, ind_b, ind_e,
    b_dense, a_dense, total, give, take, ready, result,
    local_sem, ind_sem, a_send, a_recv, b_send, b_recv, e_send,
    ta_send, ta_recv, tb_send, tb_recv, te_recv, x_send, x_recv, o_send, o_recv,
):
    r = lax.axis_index("row")
    c = lax.axis_index("col")
    d = lax.axis_index("depth")
    n = 4
    slots_a, side = a_hbm.shape[0], a_hbm.shape[1]
    slots_b = b_hbm.shape[0]
    half_b = slots_b // 2
    rows = side // NCH
    mine = out.shape[0]
    x, y = r % 2, r // 2
    across = (y * 2 + (1 - x), (1 - y) * 2 + x)
    corner = (1 - y) * 2 + (1 - x)
    mate = c + 1 - 2 * (c % 2)
    inner = (c == 1) | (c == 2)
    is_end = (c == 0) | (c == 3)
    opposite = 3 - c
    far_end = 3 - mate

    barrier = pltpu.get_barrier_semaphore()
    z_peers = [(c + s) % n for s in range(1, n)]
    r_peers = [(r + s) % n for s in range(1, n)]
    for z in z_peers:
        pl.semaphore_signal(barrier, inc=1, device_id=(r, z, d), device_id_type=MESH)
    for q in r_peers:
        pl.semaphore_signal(barrier, inc=1, device_id=(q, c, d), device_id_type=MESH)
        pl.semaphore_signal(barrier, inc=1, device_id=(q, mate, d), device_id_type=MESH)
    pl.semaphore_signal(barrier, inc=1, device_id=(r, c, 1 - d), device_id_type=MESH)

    load_a = pltpu.make_async_copy(a_hbm, own.at[pl.ds(0, slots_a)], local_sem.at[0])
    load_b = pltpu.make_async_copy(b_hbm, b_mine.at[r, pl.ds(0, slots_b)], local_sem.at[1])
    load_a.start()
    load_b.start()

    lane = lax.broadcasted_iota(jnp.int32, (8, 128), 1)
    line = lax.broadcasted_iota(jnp.int32, (8, 128), 0)
    inv_a = jnp.full((8, 128), slots_a, jnp.int32)
    for s in range(slots_a):
        inv_a = jnp.where((lane == a_idx[s]) & (s < a_cnt[0]), s, inv_a)
    goals = jnp.zeros((8, 128), jnp.int32)
    for t in range(2 * mine):
        goals = jnp.where(lane == t, c_idx[t], goals)
    inv_b = jnp.full((8, 128), slots_b, jnp.int32)
    for s in range(slots_b):
        inv_b = jnp.where((lane == b_idx[s]) & (s < b_cnt[0]), s, inv_b)
    tab_a[c] = jnp.where(line == 1, goals, inv_a)
    tab_b[r] = inv_b

    def a_copy(kind, h):
        at = (pl.ds(0, slots_a), pl.ds(h * rows, rows))
        if kind == 0:
            source, target, to = own.at[at], near.at[at], mate
        elif kind == 1:
            source, target, to = own.at[at], other.at[at], opposite
        else:
            source, target, to = near.at[at], far[h].at[pl.ds(0, slots_a)], opposite
        return pltpu.make_async_remote_copy(
            src_ref=source, dst_ref=target,
            send_sem=a_send.at[kind, h], recv_sem=a_recv.at[kind, h],
            device_id=(r, to, d), device_id_type=MESH,
        )

    columns = (b_mine, b_mate)

    def b_copy(column, source, half, way, k):
        part = columns[column].at[source, pl.ds(half * half_b, half_b)]
        return pltpu.make_async_remote_copy(
            src_ref=part, dst_ref=part,
            send_sem=b_send.at[column, way, k], recv_sem=b_recv.at[column, source, half],
            device_id=(across[way], c, d), device_id_type=MESH,
        )

    def e_copy(half):
        at = pl.ds(half * half_b, half_b)
        return pltpu.make_async_remote_copy(
            src_ref=b_mine.at[r, at], dst_ref=b_mate.at[r, at],
            send_sem=e_send.at[half], recv_sem=b_recv.at[1, r, half],
            device_id=(r, mate, d), device_id_type=MESH,
        )

    def ta_copy(source, to, k):
        return pltpu.make_async_remote_copy(
            src_ref=tab_a.at[source], dst_ref=tab_a.at[source],
            send_sem=ta_send.at[k], recv_sem=ta_recv.at[source],
            device_id=(r, to, d), device_id_type=MESH,
        )

    def tb_copy(source, to, k):
        return pltpu.make_async_remote_copy(
            src_ref=tab_b.at[source], dst_ref=tab_b.at[source],
            send_sem=tb_send.at[k], recv_sem=tb_recv.at[source],
            device_id=(to, c, d), device_id_type=MESH,
        )

    def te_copy(source, to, k):
        return pltpu.make_async_remote_copy(
            src_ref=tab_b.at[source], dst_ref=tab_e.at[source],
            send_sem=tb_send.at[k], recv_sem=te_recv.at[source],
            device_id=(to, mate, d), device_id_type=MESH,
        )

    def x_copy(column, h):
        return pltpu.make_async_remote_copy(
            src_ref=give.at[column, h], dst_ref=take.at[column, h],
            send_sem=x_send.at[column, h], recv_sem=x_recv.at[column, h],
            device_id=(r, c, 1 - d), device_id_type=MESH,
        )

    def o_copy(h):
        return pltpu.make_async_remote_copy(
            src_ref=ready.at[h], dst_ref=result.at[h],
            send_sem=o_send.at[h], recv_sem=o_recv.at[h],
            device_id=(r, mate, d), device_id_type=MESH,
        )

    load_a.wait()
    load_b.wait()
    pl.semaphore_wait(barrier, 10)

    @pl.when(is_end)
    def _():
        e_copy(0).start()
        e_copy(1).start()
        for q in range(n):
            te_copy(r, (r + q) % n, q).start()
        ta_copy(c, mate, 0).start()
        ta_copy(c, 3 - mate, 1).start()
        for h in range(NCH):
            a_copy(0, h).start()
        for h in range(NCH):
            o_copy(h).wait_recv()
            for t in range(mine):
                out[t, pl.ds(h * rows, rows)] = result[h, t]
        for h in range(NCH):
            a_copy(0, h).wait_send()
        for half in range(2):
            e_copy(half).wait_send()
        for q in range(n):
            te_copy(r, r, q).wait_send()
        for k in range(2):
            ta_copy(c, mate, k).wait_send()

    def expand_b(column, source):
        place = c if column == 0 else mate
        partner = (r + source - place + n) % n
        held, index = columns[column], (ind_b, ind_e)[column]

        def one(q, carry):
            for j in range(CB):
                b_dense[
                    column, j // 2, pl.ds(pl.multiple_of(q * side, side), side), pl.ds(j % 2 * side, side)
                ] = held[partner, index[partner, 0, q * CB + j]]
            return carry

        lax.fori_loop(0, KB, one, 0)

    def expand_a(k, ref, source):
        height = ref.shape[1]
        for i in range(RB):
            for q in range(KB):
                a_dense[k, pl.ds(i * height, height), pl.ds(q * side, side)] = ref[
                    ind_a[source, 0, i * KB + q]
                ]

    def multiply(column, k, height, h):
        at = pl.ds(h * height, height)

        def one(t, carry):
            got = jnp.dot(
                a_dense[k, pl.ds(0, RB * height)], b_dense[column, t],
                preferred_element_type=jnp.float32,
            )
            for i in range(RB):
                for j in range(2):
                    total[column, i * CB + t * 2 + j, at] += got[
                        i * height : (i + 1) * height, j * side : (j + 1) * side
                    ]
            return carry

        lax.fori_loop(0, CB // 2, one, 0)

    def b_first(column):
        b_copy(column, r, 0, 0, 0).start()
        b_copy(column, r, 1, 1, 0).start()
        b_copy(column, r, 1, 0, 1).start()
        b_copy(column, r, 0, 1, 1).start()

    def b_onward(column):
        b_copy(column, across[0], 0, 1, 2).wait_recv()
        b_copy(column, across[0], 0, 1, 2).start()
        b_copy(column, across[1], 1, 0, 2).wait_recv()
        b_copy(column, across[1], 1, 0, 2).start()

    def b_rest(column):
        b_copy(column, across[0], 1, 0, 0).wait_recv()
        b_copy(column, across[1], 0, 0, 0).wait_recv()
        b_copy(column, corner, 0, 0, 0).wait_recv()
        b_copy(column, corner, 1, 0, 0).wait_recv()

    def relay(h):
        a_copy(0, h).wait_recv()
        a_copy(2, h).start()

    def finish(h):
        at = pl.ds(h * rows, rows)
        x_copy(1, h).wait_recv()
        for t in range(mine):
            ready[h, t] = (total[1, ind_a[mate, 1, d * mine + t], at] + take[1, h, t]).astype(out.dtype)
        o_copy(h).start()
        x_copy(0, h).wait_recv()
        for t in range(mine):
            out[t, at] = (total[0, c_idx[d * mine + t], at] + take[0, h, t]).astype(out.dtype)

    @pl.when(inner)
    def _():
        for s in range(n - 1):
            tb_copy(r, r_peers[s], s).start()
        ta_copy(c, opposite, 0).start()
        b_first(0)
        for h in range(NCH):
            a_copy(1, h).start()

        for p in range(n):
            b_mine[p, slots_b] = jnp.zeros((side, side), b_mine.dtype)
            b_mate[p, slots_b] = jnp.zeros((side, side), b_mate.dtype)
        for ref in (own, near, other):
            ref[slots_a] = jnp.zeros((side, side), ref.dtype)
        for ref in far:
            ref[slots_a] = jnp.zeros((rows, side), ref.dtype)

        def zero(t, carry):
            total[0, t] = jnp.zeros((side, side), jnp.float32)
            total[1, t] = jnp.zeros((side, side), jnp.float32)
            return carry

        lax.fori_loop(0, RB * CB, zero, 0)

        for s in range(n - 1):
            ta_copy(z_peers[s], opposite, 0).wait_recv()
            tb_copy(r_peers[s], r, 0).wait_recv()
        for q in range(n):
            te_copy(q, r, 0).wait_recv()
        fetches = [
            pltpu.make_async_copy(tab, ind, ind_sem.at[k])
            for k, (tab, ind) in enumerate(((tab_a, ind_a), (tab_b, ind_b), (tab_e, ind_e)))
        ]
        for fetch in fetches:
            fetch.start()
        for fetch in fetches:
            fetch.wait()
        expand_a(0, own, c)

        b_onward(0)
        e_copy(0).wait_recv()
        e_copy(1).wait_recv()
        b_first(1)
        relay(0)
        b_rest(0)
        expand_b(0, c)
        multiply(0, 0, side, 0)
        relay(1)
        for h in range(NCH):
            a_copy(1, h).wait_recv()
        expand_a(1, other, opposite)
        expand_b(0, opposite)
        multiply(0, 1, side, 0)
        b_onward(1)
        for h in range(2, NCH):
            relay(h)
        expand_a(2, near, mate)
        expand_b(0, mate)
        multiply(0, 2, side, 0)
        expand_b(0, far_end)
        b_rest(1)
        for k, source in enumerate((c, opposite, mate)):
            expand_b(1, source)
            multiply(1, k, side, 0)
        expand_b(1, far_end)

        for h in range(NCH):
            at = pl.ds(h * rows, rows)
            a_copy(2, h).wait_recv()
            expand_a(0, far[h], far_end)
            multiply(1, 0, rows, h)
            for t in range(mine):
                give[1, h, t] = total[1, ind_a[mate, 1, (1 - d) * mine + t], at]
            x_copy(1, h).start()
            multiply(0, 0, rows, h)
            for t in range(mine):
                give[0, h, t] = total[0, c_idx[(1 - d) * mine + t], at]
            x_copy(0, h).start()
            if h > 0 and h < NCH - 1:
                finish(h - 1)
            elif h == NCH - 1:
                finish(h - 1)
                finish(h)

        for h in range(NCH):
            for column in range(2):
                x_copy(column, h).wait_send()
            a_copy(1, h).wait_send()
            a_copy(2, h).wait_send()
            o_copy(h).wait_send()
        for column in range(2):
            for way in range(2):
                for k in range(3):
                    b_copy(column, r, 0, way, k).wait_send()
        for s in range(n - 1):
            tb_copy(r, r, s).wait_send()
        ta_copy(c, opposite, 0).wait_send()


def fast_body(left_block_slots, a_index, a_count, b_blocks, b_index, b_count, c_index):
    slots_a, side = left_block_slots.shape[4], left_block_slots.shape[5]
    slots_b = b_blocks.shape[4]
    targets = c_index.shape[2]
    mine = targets // 2
    n = 4
    bf, f32, i32 = jnp.bfloat16, jnp.float32, jnp.int32
    rows = side // NCH
    dma = pltpu.SemaphoreType.DMA
    smem = pl.BlockSpec(memory_space=pltpu.SMEM)
    hbm = pl.BlockSpec(memory_space=pl.ANY)
    flops = 2 * RB * KB * CB * side**3 * n
    out = pl.pallas_call(
        fast_kernel,
        out_shape=jax.ShapeDtypeStruct((mine, side, side), bf),
        in_specs=[hbm, hbm, smem, smem, smem, smem, smem],
        out_specs=pl.BlockSpec(memory_space=pltpu.VMEM),
        scratch_shapes=[
            pltpu.VMEM((slots_a + 1, side, side), bf),
            pltpu.VMEM((slots_a + 1, side, side), bf),
            pltpu.VMEM((slots_a + 1, side, side), bf),
            tuple(pltpu.VMEM((slots_a + 1, rows, side), bf) for h in range(NCH)),
            pltpu.VMEM((n, slots_b + 1, side, side), bf),
            pltpu.VMEM((n, slots_b + 1, side, side), bf),
            pltpu.VMEM((n, 8, 128), i32),
            pltpu.VMEM((n, 8, 128), i32),
            pltpu.VMEM((n, 8, 128), i32),
            pltpu.SMEM((n, 8, 128), i32),
            pltpu.SMEM((n, 8, 128), i32),
            pltpu.SMEM((n, 8, 128), i32),
            pltpu.VMEM((2, CB // 2, KB * side, 2 * side), bf),
            pltpu.VMEM((3, RB * side, KB * side), bf),
            pltpu.VMEM((2, RB * CB, side, side), f32),
            pltpu.VMEM((2, NCH, mine, rows, side), f32),
            pltpu.VMEM((2, NCH, mine, rows, side), f32),
            pltpu.VMEM((NCH, mine, rows, side), bf),
            pltpu.VMEM((NCH, mine, rows, side), bf),
            dma((2,)),
            dma((3,)),
            dma((3, NCH)),
            dma((3, NCH)),
            dma((2, 2, 3)),
            dma((2, n, 2)),
            dma((2,)),
            dma((2,)),
            dma((n,)),
            dma((n,)),
            dma((n,)),
            dma((n,)),
            dma((2, NCH)),
            dma((2, NCH)),
            dma((NCH,)),
            dma((NCH,)),
        ],
        compiler_params=pltpu.CompilerParams(
            collective_id=0, has_side_effects=True, vmem_limit_bytes=40 * 1024 * 1024
        ),
        cost_estimate=pl.CostEstimate(flops=flops, bytes_accessed=4 << 20, transcendentals=0),
    )(
        left_block_slots[0, 0, 0, 0],
        b_blocks[0, 0, 0, 0],
        a_index[0, 0, 0, 0],
        a_count[0, 0, 0],
        b_index[0, 0, 0, 0],
        b_count[0, 0, 0],
        c_index[0, 0],
    )
    return out[None, None]


def solution(mesh):
    placed = (
        P("row", "col", "depth", None, None, None, None),
        P("row", "col", "depth", None, None),
        P("row", "col", "depth", None),
        P("row", "col", "depth", None, None, None, None),
        P("row", "col", "depth", None, None),
        P("row", "col", "depth", None),
        P("row", "col", None),
    )
    square = (mesh.shape["row"], mesh.shape["col"], mesh.shape["depth"]) == (4, 4, 2)
    return jax.shard_map(
        fast_body if square else body,
        mesh=mesh,
        in_specs=placed,
        out_specs=P("row", "col", "depth", None, None),
        check_vma=False,
    )
```

```python
import jax
import jax.numpy as jnp
from jax import lax
from jax.experimental import pallas as pl
from jax.experimental.pallas import tpu as pltpu
from jax.sharding import PartitionSpec as P

RB = 4
KB = 8
CB = 8
NCH = 4
MESH = pl.DeviceIdType.MESH


def from_behind(value, axis, steps):
    count = lax.axis_size(axis)
    pairs = [(source, (source + steps) % count) for source in range(count)]
    return lax.ppermute(value, axis, pairs)


def select_blocks(blocks, positions, count, wanted):
    slots = blocks.shape[0]
    side = blocks.shape[-1]
    live = jnp.arange(slots, dtype=jnp.int32) < count
    picker = ((wanted.reshape(-1)[:, None] == positions[None, :]) & live[None, :]).astype(
        jnp.bfloat16
    )
    flat = blocks.reshape(slots, side * side)
    chosen = jnp.dot(picker, flat, preferred_element_type=jnp.float32).astype(jnp.bfloat16)
    return chosen.reshape(wanted.shape + (side, side))


def contribute(product_total, left_portion, b_part, left_pick, right_pick):
    left_strip = select_blocks(left_portion[0], left_portion[1], left_portion[2], left_pick)
    right_strip = select_blocks(b_part[0], b_part[1], b_part[2], right_pick)
    return product_total + jnp.einsum(
        "oxmn,oxnw->omw", left_strip, right_strip, preferred_element_type=jnp.float32
    )


def pick(held, index):
    return tuple((lax.dynamic_index_in_dim(member, index, 0, keepdims=False) for member in held))


def window(held, leading, slot_count):
    chosen = jnp.stack(
        [
            jnp.asarray(leading, jnp.int32) % slot_count,
            (jnp.asarray(leading, jnp.int32) + 1) % slot_count,
        ]
    )
    return tuple((jnp.take(member, chosen, axis=0) for member in held))


def body(left_block_slots, a_index, a_count, b_blocks, b_index, b_count, c_index):
    row_pos = lax.axis_index("row")
    n_row = lax.axis_size("row")
    n_col = lax.axis_size("col")
    span = max(n_row, n_col)
    a_slots = left_block_slots.shape[3]
    b_slots = b_blocks.shape[3]
    rounds = max(a_slots, b_slots)
    length = span // rounds
    targets = c_index[0, 0]
    rows_t = targets // CB
    cols_t = targets % CB
    inner_cols = jnp.arange(KB, dtype=jnp.int32)
    left_pick = rows_t[:, None] * KB + inner_cols[None, :]
    right_pick = inner_cols[None, :] * CB + cols_t[:, None]
    a_held = (left_block_slots[0, 0, 0], a_index[0, 0, 0], a_count[0, 0, 0])
    b_held = (b_blocks[0, 0, 0], b_index[0, 0, 0], b_count[0, 0, 0])

    def a_use(held):
        return pick(held, 0)

    def a_move(held):
        return tuple(from_behind((held[0], held[1], held[2]), "col", -1))

    def a_end(held):
        return a_move(held)

    def b_begin(held, rnd):
        if b_slots > 1:
            return window(b_held, rnd, b_slots)
        return held

    def b_use(held, step):
        if b_slots > 1:
            return pick(held, (row_pos + step) // n_row)
        return pick(held, 0)

    def right_shifted(held):
        return tuple(from_behind((held[0], held[1], held[2]), "row", -1))

    def b_end(held):
        if b_slots == 1:
            return right_shifted(held)
        return held

    b_start = b_begin(b_held, 0)

    def run_round(rnd, a_now, b_now, product_total):
        a_now = tuple(a_now)
        b_now = tuple(b_begin(b_now, rnd))

        def inner(step, carry):
            a_cur, b_cur, acc = carry
            acc = contribute(acc, a_use(a_cur), b_use(b_cur, step), left_pick, right_pick)
            return (tuple(a_move(a_cur)), tuple(right_shifted(b_cur)), acc)

        a_now, b_now, product_total = lax.fori_loop(
            0, length - 1, inner, (a_now, b_now, product_total)
        )
        product_total = contribute(
            product_total, a_use(a_now), b_use(b_now, length - 1), left_pick, right_pick
        )
        return (a_now, b_now, product_total)

    def full_round(rnd, carry):
        a_now, b_now, product_total = run_round(rnd, carry[0], carry[1], carry[2])
        return (tuple(a_end(a_now)), tuple(b_end(b_now)), product_total)

    side = left_block_slots.shape[-1]
    start = jnp.zeros((targets.shape[0], side, side), jnp.float32)
    a_last, b_last, product_total = lax.fori_loop(
        0, rounds - 1, full_round, (tuple(a_held), tuple(b_start), start)
    )
    a_last, b_last, product_total = run_round(rounds - 1, a_last, b_last, product_total)
    shares = lax.psum_scatter(product_total, "depth", scatter_dimension=0, tiled=True)
    return shares.astype(jnp.bfloat16)[None, None]


def fast_kernel(
    a_hbm, b_hbm, a_idx, a_cnt, b_idx, b_cnt, c_idx, out,
    own, low_one, high_one, two, far_parts, b_all, tab_a, tab_b, ind_a, ind_b, b_dense, a_dense, total, give, take,
    local_sem, ind_sem, a_send, a_recv, b_send, b_recv,
    ta_send, ta_recv, tb_send, tb_recv, x_send, x_recv,
):
    r = lax.axis_index("row")
    c = lax.axis_index("col")
    d = lax.axis_index("depth")
    n = 4
    slots_a, side = a_hbm.shape[0], a_hbm.shape[1]
    slots_b = b_hbm.shape[0]
    half_b = slots_b // 2
    rows = side // NCH
    mine = out.shape[0]
    x, y = r % 2, r // 2
    across = (y * 2 + (1 - x), (1 - y) * 2 + x)
    corner = (1 - y) * 2 + (1 - x)

    barrier = pltpu.get_barrier_semaphore()
    z_peers = [(c + s) % n for s in range(1, n)]
    r_peers = [(r + s) % n for s in range(1, n)]
    for z in z_peers:
        pl.semaphore_signal(barrier, inc=1, device_id=(r, z, d), device_id_type=MESH)
    for q in r_peers:
        pl.semaphore_signal(barrier, inc=1, device_id=(q, c, d), device_id_type=MESH)
    pl.semaphore_signal(barrier, inc=1, device_id=(r, c, 1 - d), device_id_type=MESH)

    load_a = pltpu.make_async_copy(a_hbm, own.at[pl.ds(0, slots_a)], local_sem.at[0])
    load_b = pltpu.make_async_copy(b_hbm, b_all.at[r, pl.ds(0, slots_b)], local_sem.at[1])
    load_a.start()
    load_b.start()

    lane = lax.broadcasted_iota(jnp.int32, (8, 128), 1)
    inv_a = jnp.full((8, 128), slots_a, jnp.int32)
    for s in range(slots_a):
        inv_a = jnp.where((lane == a_idx[s]) & (s < a_cnt[0]), s, inv_a)
    inv_b = jnp.full((8, 128), slots_b, jnp.int32)
    for s in range(slots_b):
        inv_b = jnp.where((lane == b_idx[s]) & (s < b_cnt[0]), s, inv_b)
    tab_a[c] = inv_a
    tab_b[r] = inv_b
    for p in range(n):
        b_all[p, slots_b] = jnp.zeros((side, side), b_all.dtype)
    for panel_ref in (own, low_one, high_one, two):
        panel_ref[slots_a] = jnp.zeros((side, side), panel_ref.dtype)
    for part_ref in far_parts:
        part_ref[slots_a] = jnp.zeros((rows, side), part_ref.dtype)

    def zero(t, carry):
        total[t] = jnp.zeros((side, side), jnp.float32)
        return carry

    lax.fori_loop(0, RB * CB, zero, 0)

    held = ((own, low_one, two), (own, high_one, two))

    def piece(way, delta, h):
        if delta == n - 1:
            return far_parts[h].at[pl.ds(0, slots_a)]
        return held[way][delta].at[pl.ds(0, slots_a), pl.ds(h * rows, rows)]

    def a_copy(way, delta, h):
        return pltpu.make_async_remote_copy(
            src_ref=piece(way, delta, h), dst_ref=piece(way, delta + 1, h),
            send_sem=a_send.at[way, delta, h], recv_sem=a_recv.at[way, delta, h],
            device_id=(r, (c + 1 - 2 * way + n) % n, d), device_id_type=MESH,
        )

    def b_copy(source, half, way, k):
        part = b_all.at[source, pl.ds(half * half_b, half_b)]
        return pltpu.make_async_remote_copy(
            src_ref=part, dst_ref=part,
            send_sem=b_send.at[way, k], recv_sem=b_recv.at[source, half],
            device_id=(across[way], c, d), device_id_type=MESH,
        )

    def ta_copy(s):
        return pltpu.make_async_remote_copy(
            src_ref=tab_a.at[c], dst_ref=tab_a.at[c],
            send_sem=ta_send.at[s], recv_sem=ta_recv.at[c],
            device_id=(r, z_peers[s], d), device_id_type=MESH,
        )

    def tb_copy(s):
        return pltpu.make_async_remote_copy(
            src_ref=tab_b.at[r], dst_ref=tab_b.at[r],
            send_sem=tb_send.at[s], recv_sem=tb_recv.at[r],
            device_id=(r_peers[s], c, d), device_id_type=MESH,
        )

    def wait_ta(source):
        pltpu.make_async_remote_copy(
            src_ref=tab_a.at[source], dst_ref=tab_a.at[source],
            send_sem=ta_send.at[0], recv_sem=ta_recv.at[source],
            device_id=(r, z_peers[0], d), device_id_type=MESH,
        ).wait_recv()

    def wait_tb(source):
        pltpu.make_async_remote_copy(
            src_ref=tab_b.at[source], dst_ref=tab_b.at[source],
            send_sem=tb_send.at[0], recv_sem=tb_recv.at[source],
            device_id=(r_peers[0], c, d), device_id_type=MESH,
        ).wait_recv()

    load_a.wait()
    load_b.wait()
    pl.semaphore_wait(barrier, 7)

    for s in range(n - 1):
        tb_copy(s).start()
        ta_copy(s).start()
    for h in range(NCH):
        if h == 0:
            b_copy(r, 0, 0, 0).start()
            b_copy(r, 1, 1, 0).start()
        if h == 1:
            b_copy(r, 1, 0, 1).start()
            b_copy(r, 0, 1, 1).start()

        @pl.when(c < n - 1)
        def _():
            a_copy(0, 0, h).start()

        @pl.when(c > 0)
        def _():
            a_copy(1, 0, h).start()

    b_copy(across[0], 0, 1, 2).wait_recv()
    b_copy(across[0], 0, 1, 2).start()
    b_copy(across[1], 1, 0, 2).wait_recv()
    b_copy(across[1], 1, 0, 2).start()

    for s in range(n - 1):
        wait_ta(z_peers[s])
        wait_tb(r_peers[s])
    fetch_a = pltpu.make_async_copy(tab_a, ind_a, ind_sem.at[0])
    fetch_b = pltpu.make_async_copy(tab_b, ind_b, ind_sem.at[1])
    fetch_a.start()
    fetch_b.start()
    fetch_a.wait()
    fetch_b.wait()

    def expand_b(source):
        partner = (r + source - c + n) % n

        def one(q, carry):
            for j in range(CB):
                block = b_all[partner, ind_b[partner, 0, q * CB + j]]
                b_dense[j // 2, pl.ds(pl.multiple_of(q * side, side), side), pl.ds(j % 2 * side, side)] = block
            return carry

        lax.fori_loop(0, KB, one, 0)

    def multiply(ref, source, h):
        height = ref.shape[1]
        at = pl.ds(h * height, height)
        for i in range(RB):
            for q in range(KB):
                a_dense[pl.ds(i * height, height), pl.ds(q * side, side)] = ref[
                    ind_a[source, 0, i * KB + q]
                ]

        def one(t, carry):
            got = jnp.dot(
                a_dense[pl.ds(0, RB * height)], b_dense[t], preferred_element_type=jnp.float32
            )
            for i in range(RB):
                for j in range(2):
                    total[i * CB + t * 2 + j, at] += got[
                        i * height : (i + 1) * height, j * side : (j + 1) * side
                    ]
            return carry

        lax.fori_loop(0, CB // 2, one, 0)

    for delta in (1, 2):
        behind = (c - delta, c + delta)
        there = (behind[0] >= 0, behind[1] < n)
        onward = (c < n - 1, c > 0)
        for h in range(NCH):
            for way in range(2):

                @pl.when(there[way])
                def _():
                    a_copy(way, delta - 1, h).wait_recv()

                    @pl.when(onward[way])
                    def _():
                        a_copy(way, delta, h).start()

        if delta == 1:
            b_copy(across[0], 1, 0, 0).wait_recv()
            b_copy(across[1], 0, 0, 0).wait_recv()
            b_copy(corner, 0, 0, 0).wait_recv()
            b_copy(corner, 1, 0, 0).wait_recv()
            expand_b(c)
            multiply(own, c, 0)
            for way in range(2):

                @pl.when(there[way])
                def _():
                    expand_b(behind[way])
                    multiply(held[way][1], behind[way], 0)

        else:
            source = jnp.where(there[0], behind[0], behind[1])
            expand_b(source)
            multiply(two, source, 0)

    far = n - 1 - c
    is_end = (c == 0) | (c == n - 1)

    @pl.when(is_end)
    def _():
        expand_b(far)

    def x_copy(h):
        return pltpu.make_async_remote_copy(
            src_ref=give.at[h], dst_ref=take.at[h],
            send_sem=x_send.at[h], recv_sem=x_recv.at[h],
            device_id=(r, c, 1 - d), device_id_type=MESH,
        )

    def finish(h):
        at = pl.ds(h * rows, rows)
        x_copy(h).wait_recv()
        for t in range(mine):
            out[t, at] = (total[c_idx[d * mine + t], at] + take[h, t]).astype(out.dtype)

    for h in range(NCH):
        at = pl.ds(h * rows, rows)
        for way in range(2):

            @pl.when(c == (n - 1) * (1 - way))
            def _():
                a_copy(way, n - 2, h).wait_recv()

        @pl.when(is_end)
        def _():
            multiply(far_parts[h], far, h)

        for t in range(mine):
            give[h, t] = total[c_idx[(1 - d) * mine + t], at]
        x_copy(h).start()
        if h > 0:
            finish(h - 1)
    finish(NCH - 1)

    for h in range(NCH):
        x_copy(h).wait_send()
        for way in range(2):
            for delta in range(n - 1):
                has = (c >= delta) & (c < n - 1) if way == 0 else (c + delta < n) & (c > 0)

                @pl.when(has)
                def _():
                    a_copy(way, delta, h).wait_send()

    for way in range(2):
        for k in range(3):
            b_copy(r, 0, way, k).wait_send()
    for s in range(n - 1):
        ta_copy(s).wait_send()
        tb_copy(s).wait_send()


def fast_body(left_block_slots, a_index, a_count, b_blocks, b_index, b_count, c_index):
    slots_a, side = left_block_slots.shape[4], left_block_slots.shape[5]
    slots_b = b_blocks.shape[4]
    targets = c_index.shape[2]
    mine = targets // 2
    n = 4
    bf, f32, i32 = jnp.bfloat16, jnp.float32, jnp.int32
    rows = side // NCH
    dma = pltpu.SemaphoreType.DMA
    smem = pl.BlockSpec(memory_space=pltpu.SMEM)
    hbm = pl.BlockSpec(memory_space=pl.ANY)
    flops = 2 * RB * KB * CB * side**3 * n
    out = pl.pallas_call(
        fast_kernel,
        out_shape=jax.ShapeDtypeStruct((mine, side, side), bf),
        in_specs=[hbm, hbm, smem, smem, smem, smem, smem],
        out_specs=pl.BlockSpec(memory_space=pltpu.VMEM),
        scratch_shapes=[
            pltpu.VMEM((slots_a + 1, side, side), bf),
            pltpu.VMEM((slots_a + 1, side, side), bf),
            pltpu.VMEM((slots_a + 1, side, side), bf),
            pltpu.VMEM((slots_a + 1, side, side), bf),
            tuple(pltpu.VMEM((slots_a + 1, rows, side), bf) for h in range(NCH)),
            pltpu.VMEM((n, slots_b + 1, side, side), bf),
            pltpu.VMEM((n, 8, 128), i32),
            pltpu.VMEM((n, 8, 128), i32),
            pltpu.SMEM((n, 8, 128), i32),
            pltpu.SMEM((n, 8, 128), i32),
            pltpu.VMEM((CB // 2, KB * side, 2 * side), bf),
            pltpu.VMEM((RB * side, KB * side), bf),
            pltpu.VMEM((RB * CB, side, side), f32),
            pltpu.VMEM((NCH, mine, rows, side), f32),
            pltpu.VMEM((NCH, mine, rows, side), f32),
            dma((2,)),
            dma((2,)),
            dma((2, n - 1, NCH)),
            dma((2, n - 1, NCH)),
            dma((2, 3)),
            dma((n, 2)),
            dma((n - 1,)),
            dma((n,)),
            dma((n - 1,)),
            dma((n,)),
            dma((NCH,)),
            dma((NCH,)),
        ],
        compiler_params=pltpu.CompilerParams(
            collective_id=0, has_side_effects=True, vmem_limit_bytes=60 * 1024 * 1024
        ),
        cost_estimate=pl.CostEstimate(flops=flops, bytes_accessed=4 << 20, transcendentals=0),
    )(
        left_block_slots[0, 0, 0, 0],
        b_blocks[0, 0, 0, 0],
        a_index[0, 0, 0, 0],
        a_count[0, 0, 0],
        b_index[0, 0, 0, 0],
        b_count[0, 0, 0],
        c_index[0, 0],
    )
    return out[None, None]


def solution(mesh):
    placed = (
        P("row", "col", "depth", None, None, None, None),
        P("row", "col", "depth", None, None),
        P("row", "col", "depth", None),
        P("row", "col", "depth", None, None, None, None),
        P("row", "col", "depth", None, None),
        P("row", "col", "depth", None),
        P("row", "col", None),
    )
    square = (mesh.shape["row"], mesh.shape["col"], mesh.shape["depth"]) == (4, 4, 2)
    return jax.shard_map(
        fast_body if square else body,
        mesh=mesh,
        in_specs=placed,
        out_specs=P("row", "col", "depth", None, None),
        check_vma=False,
    )
```

```python
import jax
import jax.numpy as jnp
from jax import lax
from jax.experimental import pallas as pl
from jax.experimental.pallas import tpu as pltpu
from jax.sharding import PartitionSpec as P

RB = 4
KB = 8
CB = 8
NCH = 8
MESH = pl.DeviceIdType.MESH


def from_behind(value, axis, steps):
    count = lax.axis_size(axis)
    pairs = [(source, (source + steps) % count) for source in range(count)]
    return lax.ppermute(value, axis, pairs)


def select_blocks(blocks, positions, count, wanted):
    slots = blocks.shape[0]
    side = blocks.shape[-1]
    live = jnp.arange(slots, dtype=jnp.int32) < count
    picker = ((wanted.reshape(-1)[:, None] == positions[None, :]) & live[None, :]).astype(
        jnp.bfloat16
    )
    flat = blocks.reshape(slots, side * side)
    chosen = jnp.dot(picker, flat, preferred_element_type=jnp.float32).astype(jnp.bfloat16)
    return chosen.reshape(wanted.shape + (side, side))


def contribute(product_total, left_portion, b_part, left_pick, right_pick):
    left_strip = select_blocks(left_portion[0], left_portion[1], left_portion[2], left_pick)
    right_strip = select_blocks(b_part[0], b_part[1], b_part[2], right_pick)
    return product_total + jnp.einsum(
        "oxmn,oxnw->omw", left_strip, right_strip, preferred_element_type=jnp.float32
    )


def pick(held, index):
    return tuple((lax.dynamic_index_in_dim(member, index, 0, keepdims=False) for member in held))


def window(held, leading, slot_count):
    chosen = jnp.stack(
        [
            jnp.asarray(leading, jnp.int32) % slot_count,
            (jnp.asarray(leading, jnp.int32) + 1) % slot_count,
        ]
    )
    return tuple((jnp.take(member, chosen, axis=0) for member in held))


def body(left_block_slots, a_index, a_count, b_blocks, b_index, b_count, c_index):
    row_pos = lax.axis_index("row")
    n_row = lax.axis_size("row")
    n_col = lax.axis_size("col")
    span = max(n_row, n_col)
    a_slots = left_block_slots.shape[3]
    b_slots = b_blocks.shape[3]
    rounds = max(a_slots, b_slots)
    length = span // rounds
    targets = c_index[0, 0]
    rows_t = targets // CB
    cols_t = targets % CB
    inner_cols = jnp.arange(KB, dtype=jnp.int32)
    left_pick = rows_t[:, None] * KB + inner_cols[None, :]
    right_pick = inner_cols[None, :] * CB + cols_t[:, None]
    a_held = (left_block_slots[0, 0, 0], a_index[0, 0, 0], a_count[0, 0, 0])
    b_held = (b_blocks[0, 0, 0], b_index[0, 0, 0], b_count[0, 0, 0])

    def a_use(held):
        return pick(held, 0)

    def a_move(held):
        return tuple(from_behind((held[0], held[1], held[2]), "col", -1))

    def a_end(held):
        return a_move(held)

    def b_begin(held, rnd):
        if b_slots > 1:
            return window(b_held, rnd, b_slots)
        return held

    def b_use(held, step):
        if b_slots > 1:
            return pick(held, (row_pos + step) // n_row)
        return pick(held, 0)

    def right_shifted(held):
        return tuple(from_behind((held[0], held[1], held[2]), "row", -1))

    def b_end(held):
        if b_slots == 1:
            return right_shifted(held)
        return held

    b_start = b_begin(b_held, 0)

    def run_round(rnd, a_now, b_now, product_total):
        a_now = tuple(a_now)
        b_now = tuple(b_begin(b_now, rnd))

        def inner(step, carry):
            a_cur, b_cur, acc = carry
            acc = contribute(acc, a_use(a_cur), b_use(b_cur, step), left_pick, right_pick)
            return (tuple(a_move(a_cur)), tuple(right_shifted(b_cur)), acc)

        a_now, b_now, product_total = lax.fori_loop(
            0, length - 1, inner, (a_now, b_now, product_total)
        )
        product_total = contribute(
            product_total, a_use(a_now), b_use(b_now, length - 1), left_pick, right_pick
        )
        return (a_now, b_now, product_total)

    def full_round(rnd, carry):
        a_now, b_now, product_total = run_round(rnd, carry[0], carry[1], carry[2])
        return (tuple(a_end(a_now)), tuple(b_end(b_now)), product_total)

    side = left_block_slots.shape[-1]
    start = jnp.zeros((targets.shape[0], side, side), jnp.float32)
    a_last, b_last, product_total = lax.fori_loop(
        0, rounds - 1, full_round, (tuple(a_held), tuple(b_start), start)
    )
    a_last, b_last, product_total = run_round(rounds - 1, a_last, b_last, product_total)
    shares = lax.psum_scatter(product_total, "depth", scatter_dimension=0, tiled=True)
    return shares.astype(jnp.bfloat16)[None, None]


def fast_kernel(
    a_hbm, b_hbm, a_idx, a_cnt, b_idx, b_cnt, c_idx, out,
    own, low_one, high_one, two, far_parts, b_all, tab_a, tab_b, ind_a, ind_b, b_dense, a_dense, total, give, take,
    local_sem, ind_sem, a_send, a_recv, b_send, b_recv,
    ta_send, ta_recv, tb_send, tb_recv, x_send, x_recv,
):
    r = lax.axis_index("row")
    c = lax.axis_index("col")
    d = lax.axis_index("depth")
    n = 4
    slots_a, side = a_hbm.shape[0], a_hbm.shape[1]
    slots_b = b_hbm.shape[0]
    half_b = slots_b // 2
    rows = side // NCH
    mine = out.shape[0]
    x, y = r % 2, r // 2
    across = (y * 2 + (1 - x), (1 - y) * 2 + x)
    corner = (1 - y) * 2 + (1 - x)

    barrier = pltpu.get_barrier_semaphore()
    z_peers = [(c + s) % n for s in range(1, n)]
    r_peers = [(r + s) % n for s in range(1, n)]
    for z in z_peers:
        pl.semaphore_signal(barrier, inc=1, device_id=(r, z, d), device_id_type=MESH)
    for q in r_peers:
        pl.semaphore_signal(barrier, inc=1, device_id=(q, c, d), device_id_type=MESH)
    pl.semaphore_signal(barrier, inc=1, device_id=(r, c, 1 - d), device_id_type=MESH)

    load_a = pltpu.make_async_copy(a_hbm, own.at[pl.ds(0, slots_a)], local_sem.at[0])
    load_b = pltpu.make_async_copy(b_hbm, b_all.at[r, pl.ds(0, slots_b)], local_sem.at[1])
    load_a.start()
    load_b.start()

    lane = lax.broadcasted_iota(jnp.int32, (8, 128), 1)
    inv_a = jnp.full((8, 128), slots_a, jnp.int32)
    for s in range(slots_a):
        inv_a = jnp.where((lane == a_idx[s]) & (s < a_cnt[0]), s, inv_a)
    inv_b = jnp.full((8, 128), slots_b, jnp.int32)
    for s in range(slots_b):
        inv_b = jnp.where((lane == b_idx[s]) & (s < b_cnt[0]), s, inv_b)
    tab_a[c] = inv_a
    tab_b[r] = inv_b
    for p in range(n):
        b_all[p, slots_b] = jnp.zeros((side, side), b_all.dtype)
    for panel_ref in (own, low_one, high_one, two):
        panel_ref[slots_a] = jnp.zeros((side, side), panel_ref.dtype)
    for part_ref in far_parts:
        part_ref[slots_a] = jnp.zeros((rows, side), part_ref.dtype)

    def zero(t, carry):
        total[t] = jnp.zeros((side, side), jnp.float32)
        return carry

    lax.fori_loop(0, RB * CB, zero, 0)

    held = ((own, low_one, two), (own, high_one, two))

    def piece(way, delta, h):
        if delta == n - 1:
            return far_parts[h].at[pl.ds(0, slots_a)]
        return held[way][delta].at[pl.ds(0, slots_a), pl.ds(h * rows, rows)]

    def a_copy(way, delta, h):
        return pltpu.make_async_remote_copy(
            src_ref=piece(way, delta, h), dst_ref=piece(way, delta + 1, h),
            send_sem=a_send.at[way, delta, h], recv_sem=a_recv.at[way, delta, h],
            device_id=(r, (c + 1 - 2 * way + n) % n, d), device_id_type=MESH,
        )

    def b_copy(source, half, way, k):
        part = b_all.at[source, pl.ds(half * half_b, half_b)]
        return pltpu.make_async_remote_copy(
            src_ref=part, dst_ref=part,
            send_sem=b_send.at[way, k], recv_sem=b_recv.at[source, half],
            device_id=(across[way], c, d), device_id_type=MESH,
        )

    def ta_copy(s):
        return pltpu.make_async_remote_copy(
            src_ref=tab_a.at[c], dst_ref=tab_a.at[c],
            send_sem=ta_send.at[s], recv_sem=ta_recv.at[c],
            device_id=(r, z_peers[s], d), device_id_type=MESH,
        )

    def tb_copy(s):
        return pltpu.make_async_remote_copy(
            src_ref=tab_b.at[r], dst_ref=tab_b.at[r],
            send_sem=tb_send.at[s], recv_sem=tb_recv.at[r],
            device_id=(r_peers[s], c, d), device_id_type=MESH,
        )

    def wait_ta(source):
        pltpu.make_async_remote_copy(
            src_ref=tab_a.at[source], dst_ref=tab_a.at[source],
            send_sem=ta_send.at[0], recv_sem=ta_recv.at[source],
            device_id=(r, z_peers[0], d), device_id_type=MESH,
        ).wait_recv()

    def wait_tb(source):
        pltpu.make_async_remote_copy(
            src_ref=tab_b.at[source], dst_ref=tab_b.at[source],
            send_sem=tb_send.at[0], recv_sem=tb_recv.at[source],
            device_id=(r_peers[0], c, d), device_id_type=MESH,
        ).wait_recv()

    load_a.wait()
    load_b.wait()
    pl.semaphore_wait(barrier, 7)

    for s in range(n - 1):
        tb_copy(s).start()
        ta_copy(s).start()
    for h in range(NCH):
        if h == 0:
            b_copy(r, 0, 0, 0).start()
            b_copy(r, 1, 1, 0).start()
        if h == 1:
            b_copy(r, 1, 0, 1).start()
            b_copy(r, 0, 1, 1).start()

        @pl.when(c < n - 1)
        def _():
            a_copy(0, 0, h).start()

        @pl.when(c > 0)
        def _():
            a_copy(1, 0, h).start()

    b_copy(across[0], 0, 1, 2).wait_recv()
    b_copy(across[0], 0, 1, 2).start()
    b_copy(across[1], 1, 0, 2).wait_recv()
    b_copy(across[1], 1, 0, 2).start()

    for s in range(n - 1):
        wait_ta(z_peers[s])
        wait_tb(r_peers[s])
    fetch_a = pltpu.make_async_copy(tab_a, ind_a, ind_sem.at[0])
    fetch_b = pltpu.make_async_copy(tab_b, ind_b, ind_sem.at[1])
    fetch_a.start()
    fetch_b.start()
    fetch_a.wait()
    fetch_b.wait()

    def expand_b(source):
        partner = (r + source - c + n) % n

        def one(q, carry):
            for j in range(CB):
                block = b_all[partner, ind_b[partner, 0, q * CB + j]]
                b_dense[j // 2, pl.ds(pl.multiple_of(q * side, side), side), pl.ds(j % 2 * side, side)] = block
            return carry

        lax.fori_loop(0, KB, one, 0)

    def multiply(ref, source, h):
        height = ref.shape[1]
        at = pl.ds(h * height, height)
        for i in range(RB):
            for q in range(KB):
                a_dense[pl.ds(i * height, height), pl.ds(q * side, side)] = ref[
                    ind_a[source, 0, i * KB + q]
                ]

        def one(t, carry):
            got = jnp.dot(
                a_dense[pl.ds(0, RB * height)], b_dense[t], preferred_element_type=jnp.float32
            )
            for i in range(RB):
                for j in range(2):
                    total[i * CB + t * 2 + j, at] += got[
                        i * height : (i + 1) * height, j * side : (j + 1) * side
                    ]
            return carry

        lax.fori_loop(0, CB // 2, one, 0)

    for delta in (1, 2):
        behind = (c - delta, c + delta)
        there = (behind[0] >= 0, behind[1] < n)
        onward = (c < n - 1, c > 0)
        for h in range(NCH):
            for way in range(2):

                @pl.when(there[way])
                def _():
                    a_copy(way, delta - 1, h).wait_recv()

                    @pl.when(onward[way])
                    def _():
                        a_copy(way, delta, h).start()

        if delta == 1:
            b_copy(across[0], 1, 0, 0).wait_recv()
            b_copy(across[1], 0, 0, 0).wait_recv()
            b_copy(corner, 0, 0, 0).wait_recv()
            b_copy(corner, 1, 0, 0).wait_recv()
            expand_b(c)
            multiply(own, c, 0)
            for way in range(2):

                @pl.when(there[way])
                def _():
                    expand_b(behind[way])
                    multiply(held[way][1], behind[way], 0)

        else:
            source = jnp.where(there[0], behind[0], behind[1])
            expand_b(source)
            multiply(two, source, 0)

    far = n - 1 - c
    is_end = (c == 0) | (c == n - 1)

    @pl.when(is_end)
    def _():
        expand_b(far)

    def x_copy(h):
        return pltpu.make_async_remote_copy(
            src_ref=give.at[h], dst_ref=take.at[h],
            send_sem=x_send.at[h], recv_sem=x_recv.at[h],
            device_id=(r, c, 1 - d), device_id_type=MESH,
        )

    def finish(h):
        at = pl.ds(h * rows, rows)
        x_copy(h).wait_recv()
        for t in range(mine):
            out[t, at] = (total[c_idx[d * mine + t], at] + take[h, t]).astype(out.dtype)

    for h in range(NCH):
        at = pl.ds(h * rows, rows)
        for way in range(2):

            @pl.when(c == (n - 1) * (1 - way))
            def _():
                a_copy(way, n - 2, h).wait_recv()

        @pl.when(is_end)
        def _():
            multiply(far_parts[h], far, h)

        for t in range(mine):
            give[h, t] = total[c_idx[(1 - d) * mine + t], at]
        x_copy(h).start()
        if h > 0:
            finish(h - 1)
    finish(NCH - 1)

    for h in range(NCH):
        x_copy(h).wait_send()
        for way in range(2):
            for delta in range(n - 1):
                has = (c >= delta) & (c < n - 1) if way == 0 else (c + delta < n) & (c > 0)

                @pl.when(has)
                def _():
                    a_copy(way, delta, h).wait_send()

    for way in range(2):
        for k in range(3):
            b_copy(r, 0, way, k).wait_send()
    for s in range(n - 1):
        ta_copy(s).wait_send()
        tb_copy(s).wait_send()


def fast_body(left_block_slots, a_index, a_count, b_blocks, b_index, b_count, c_index):
    slots_a, side = left_block_slots.shape[4], left_block_slots.shape[5]
    slots_b = b_blocks.shape[4]
    targets = c_index.shape[2]
    mine = targets // 2
    n = 4
    bf, f32, i32 = jnp.bfloat16, jnp.float32, jnp.int32
    rows = side // NCH
    dma = pltpu.SemaphoreType.DMA
    smem = pl.BlockSpec(memory_space=pltpu.SMEM)
    hbm = pl.BlockSpec(memory_space=pl.ANY)
    flops = 2 * RB * KB * CB * side**3 * n
    out = pl.pallas_call(
        fast_kernel,
        out_shape=jax.ShapeDtypeStruct((mine, side, side), bf),
        in_specs=[hbm, hbm, smem, smem, smem, smem, smem],
        out_specs=pl.BlockSpec(memory_space=pltpu.VMEM),
        scratch_shapes=[
            pltpu.VMEM((slots_a + 1, side, side), bf),
            pltpu.VMEM((slots_a + 1, side, side), bf),
            pltpu.VMEM((slots_a + 1, side, side), bf),
            pltpu.VMEM((slots_a + 1, side, side), bf),
            tuple(pltpu.VMEM((slots_a + 1, rows, side), bf) for h in range(NCH)),
            pltpu.VMEM((n, slots_b + 1, side, side), bf),
            pltpu.VMEM((n, 8, 128), i32),
            pltpu.VMEM((n, 8, 128), i32),
            pltpu.SMEM((n, 8, 128), i32),
            pltpu.SMEM((n, 8, 128), i32),
            pltpu.VMEM((CB // 2, KB * side, 2 * side), bf),
            pltpu.VMEM((RB * side, KB * side), bf),
            pltpu.VMEM((RB * CB, side, side), f32),
            pltpu.VMEM((NCH, mine, rows, side), f32),
            pltpu.VMEM((NCH, mine, rows, side), f32),
            dma((2,)),
            dma((2,)),
            dma((2, n - 1, NCH)),
            dma((2, n - 1, NCH)),
            dma((2, 3)),
            dma((n, 2)),
            dma((n - 1,)),
            dma((n,)),
            dma((n - 1,)),
            dma((n,)),
            dma((NCH,)),
            dma((NCH,)),
        ],
        compiler_params=pltpu.CompilerParams(
            collective_id=0, has_side_effects=True, vmem_limit_bytes=60 * 1024 * 1024
        ),
        cost_estimate=pl.CostEstimate(flops=flops, bytes_accessed=4 << 20, transcendentals=0),
    )(
        left_block_slots[0, 0, 0, 0],
        b_blocks[0, 0, 0, 0],
        a_index[0, 0, 0, 0],
        a_count[0, 0, 0],
        b_index[0, 0, 0, 0],
        b_count[0, 0, 0],
        c_index[0, 0],
    )
    return out[None, None]


def solution(mesh):
    placed = (
        P("row", "col", "depth", None, None, None, None),
        P("row", "col", "depth", None, None),
        P("row", "col", "depth", None),
        P("row", "col", "depth", None, None, None, None),
        P("row", "col", "depth", None, None),
        P("row", "col", "depth", None),
        P("row", "col", None),
    )
    square = (mesh.shape["row"], mesh.shape["col"], mesh.shape["depth"]) == (4, 4, 2)
    return jax.shard_map(
        fast_body if square else body,
        mesh=mesh,
        in_specs=placed,
        out_specs=P("row", "col", "depth", None, None),
        check_vma=False,
    )
```
